1024 devices in a mesh: context: 64 (over x, z), dp: 2 (over y_hi), tensor: 8 (over y_lo, core).
Axes of the slice: x: 8, y: 8 (y_hi: 2, y_lo: 4; y = y_hi * 4 + y_lo), z: 8, core: 2. Of those that a mesh axis runs over, the one named last changes fastest.
Arguments:
- queries: bfloat16 [2, 16384, 8192], P('dp', 'context', 'tensor'), may hold values from -6 to 6
- keys_values: bfloat16 [2, 16384, 2048], P('dp', 'context', 'tensor'), may hold values from -6 to 6
- outputs: bfloat16 [2, 16384, 8192], P('dp', 'context', 'tensor'), may hold values from -3 to 3
- grad_out: bfloat16 [2, 16384, 8192], P('dp', 'context', 'tensor'), may hold values from -48 to 48
- logsumexp: float32 [2, 64, 16384], P('dp', 'tensor', 'context'), may hold values from 4.5 to 6.5
- doc_ids: int32 [2, 16384], P('dp'), may hold values from 0 to 3, as said below
- inputs: bfloat16 [2, 16384, 4096], P('dp', 'context'), may hold values from -0.1875 to 0.1875
Outputs:
- grad_queries: bfloat16 [2, 16384, 8192], P('dp', 'context', 'tensor')
- grad_keys_values: bfloat16 [2, 16384, 2048], P('dp', 'context', 'tensor')
- grad_value_proj: float32 [8, 4096, 128], P('tensor', ('context', 'dp'))
The draws below stay inside these ranges and needn't reach their ends.
Inputs may be any that keep to these rules, and one draw needn't show every extreme that they name: `doc_ids`: for each sequence, the ids never fall along token position pos, each of the 4 documents holds one or more tokens, and the last document holds every token from position (63) * (128) on.
All inputs are finite; a program needn't handle non-finite values.
Results may differ from the reference program's by a relative error of at most 0.0049.
Values may be sent and summed in bfloat16 or wider, within the bound.
No kernel may reach another device: no remote copies, remote signals or barrier semaphores. Data moves between devices by JAX's collectives and lax.ppermute only.
A program may use at most 32 MiB of HBM per device.

```python
import jax
import jax.numpy as jnp
from jax import lax

HD = 128
GROUP = 8
D_WIN = 4096
TOK_DEV = 256
DOCS = 4
KVH = 8
HEADS = 64
SPANS = 64
SEQ = 16384
ALL_ROWS = 32768
N_DP = 2


def draw_doc_ids(key, part):
    span_count = SEQ // TOK_DEV
    half_len = TOK_DEV // 2
    stored = jnp.arange(SEQ, dtype=jnp.int32)
    stretch = stored // TOK_DEV
    offsets = stored % TOK_DEV
    position = jnp.where(offsets < half_len, stretch * half_len + offsets, (2 * span_count - 1 - stretch) * half_len + offsets - half_len)
    cut_range = (span_count - 1) * half_len - 1

    def one_sequence(seq_key):
        cut_points = jax.random.permutation(seq_key, cut_range)[:DOCS - 1] + 1
        return jnp.sum((position[:, None] >= cut_points[None, :]).astype(jnp.int32), axis=1).astype(jnp.int32)
    seq_keys = jax.random.split(jax.random.fold_in(key, 71), N_DP)
    return jax.vmap(one_sequence)(seq_keys)


def raised(array, own_key, source, target, parts, factor):
    owner, partner = [(jnp.arange(array.shape[axis_at]) // (array.shape[axis_at] // parts)).reshape([-1 if axis == axis_at else 1 for axis in range(array.ndim)]) for axis_at in (source, target)]
    chosen = jax.random.permutation(own_key, parts)[partner]
    strong = (owner == chosen) | (owner == (partner + parts // 2) % parts)
    return jnp.where(strong, factor * array, array)


def steps_of(own_key, dims, cuts, smallest, top_value):
    gain, own = 1.0, jax.random.fold_in(own_key, 6)
    for dim, parts in cuts:
        heights = jnp.exp(jax.random.uniform(jax.random.fold_in(own, dim), (parts,), jnp.float32, smallest / len(cuts), top_value / len(cuts)))
        gain = gain * jnp.repeat(heights, dims[dim] // parts).reshape([-1 if axis == dim else 1 for axis in range(len(dims))])
    return gain


def gaussian(key, shape, spread, bound, pieces=(), kind=jnp.bfloat16):
    drawn = spread * jax.random.normal(key, shape, jnp.float32)
    if pieces:
        drawn = drawn * steps_of(key, shape, pieces, -0.22, 0.18)
    return jnp.clip(drawn, -bound, bound).astype(kind)


def gaussian_with(stream_key, shape, width, bound, cuts, heavy, kind=jnp.bfloat16):
    entries = width * jax.random.normal(stream_key, shape, jnp.float32)
    if cuts:
        entries = entries * steps_of(stream_key, shape, cuts, -0.22, 0.18)
    return jnp.clip(raised(entries, jax.random.fold_in(stream_key, 3), *heavy), -bound, bound).astype(kind)


def setup_inputs(seed: int = 0) -> dict:
    key_of = jax.random.split(jax.random.key(seed), 8)
    queries = gaussian(key_of[0], (N_DP, SEQ, HEADS * HD), 1.0, 6.0, ((0, 2), (1, 64), (2, 8)))
    keys_values = gaussian(key_of[1], (N_DP, SEQ, KVH * 2 * HD), 1.0, 6.0, ((0, 2), (1, 64), (2, 8)))
    outputs = gaussian(key_of[2], (N_DP, SEQ, HEADS * HD), 0.5, 3.0, ((0, 2), (1, 64), (2, 8)))
    grad_out = gaussian(key_of[3], (N_DP, SEQ, HEADS * HD), 8.0, 48.0, ((0, 2), (1, 64), (2, 8)))
    logsumexp = jnp.clip(4.5 + 2.0 * jax.random.uniform(key_of[4], (N_DP, HEADS, SEQ), jnp.float32) ** steps_of(key_of[4], (N_DP, HEADS, SEQ), ((0, 2), (1, 8), (2, 64)), -0.2, 0.2), 4.5, 6.5)
    doc_ids = draw_doc_ids(jax.random.fold_in(key_of[7], 71), 0)
    inputs = gaussian_with(key_of[6], (N_DP, SEQ, D_WIN), (2.0 / ALL_ROWS ** 0.5), 0.1875, ((0, 2), (1, 64)), (1, 2, 64, 4.0))
    return dict(queries=queries, keys_values=keys_values, outputs=outputs, grad_out=grad_out, logsumexp=logsumexp, doc_ids=doc_ids, inputs=inputs)


def token_positions(device, tok_rows, cycle_size):
    half_len = tok_rows // 2
    offsets = jnp.arange(tok_rows, dtype=jnp.int32)
    early = offsets < half_len
    later = (2 * cycle_size - 1 - device) * half_len + offsets - half_len
    return jnp.where(early, device * half_len + offsets, later).astype(jnp.int32)


def block_backward(query_block, key_rows, value_rows, grad_block, output_block, lse_block, visible):
    scaling = HD ** -0.5
    scores = jnp.einsum("qgd,kd->gqk", query_block.astype(jnp.float32), key_rows.astype(jnp.float32))
    attn_prob = jnp.where(visible[None], jnp.exp(scores * scaling - lse_block[:, :, None]), jnp.float32(0.0))
    row_delta = jnp.sum(grad_block.astype(jnp.float32) * output_block.astype(jnp.float32), axis=2).T
    grad_prob = jnp.einsum("qgd,kd->gqk", grad_block.astype(jnp.float32), value_rows.astype(jnp.float32))
    grad_score = attn_prob * (grad_prob - row_delta[:, :, None])
    prob_half = attn_prob.astype(jnp.bfloat16)
    score_half = grad_score.astype(jnp.bfloat16)
    value_grad = jnp.einsum("gqk,qgd->kd", prob_half.astype(jnp.float32), grad_block.astype(jnp.float32))
    key_grad = scaling * jnp.einsum("gqk,qgd->kd", score_half.astype(jnp.float32), query_block.astype(jnp.float32))
    query_grad = scaling * jnp.einsum("gqk,kd->qgd", score_half.astype(jnp.float32), key_rows.astype(jnp.float32))
    return query_grad, key_grad, value_grad


def reference(queries, keys_values, outputs, grad_out, logsumexp, doc_ids, inputs):
    proj_total = jnp.zeros((KVH, D_WIN, HD), jnp.float32)
    query_parts = []
    kv_parts = []
    for seq_index in range(N_DP):
        q_seq = queries[seq_index].reshape(SPANS, TOK_DEV, KVH, GROUP, HD)
        kv_seq = keys_values[seq_index].reshape(SPANS, TOK_DEV, KVH, 2, HD)
        out_seq = outputs[seq_index].reshape(SPANS, TOK_DEV, KVH, GROUP, HD)
        grad_seq = grad_out[seq_index].reshape(SPANS, TOK_DEV, KVH, GROUP, HD)
        lse_seq = logsumexp[seq_index].reshape(KVH, GROUP, SPANS, TOK_DEV)
        seq_docs = doc_ids[seq_index].reshape(SPANS, TOK_DEV)
        features = inputs[seq_index].reshape(SEQ, D_WIN)
        head_queries = []
        head_kv = []
        for head in range(KVH):
            def one_span(device):
                prev_dev = ((device - 1 + SPANS) % SPANS).astype(jnp.int32)
                key_rows = jnp.concatenate([kv_seq[device, :, head, 0], kv_seq[prev_dev, :, head, 0]], axis=0)
                value_rows = jnp.concatenate([kv_seq[device, :, head, 1], kv_seq[prev_dev, :, head, 1]], axis=0)
                query_pos = token_positions(device, TOK_DEV, SPANS)
                key_pos = jnp.concatenate([query_pos, token_positions(prev_dev, TOK_DEV, SPANS)])
                own_docs = seq_docs[device]
                key_docs = jnp.concatenate([own_docs, seq_docs[prev_dev]])
                visible = (key_pos[None, :] <= query_pos[:, None]) & (key_docs[None, :] == own_docs[:, None])
                return block_backward(q_seq[device, :, head], key_rows, value_rows, grad_seq[device, :, head],
                                      out_seq[device, :, head], lse_seq[head, :, device], visible)

            query_grad, key_grad, value_grad = lax.map(one_span, jnp.arange(SPANS, dtype=jnp.int32))
            key_total = key_grad[:, :TOK_DEV] + jnp.roll(key_grad[:, TOK_DEV:], -1, axis=0)
            value_total = value_grad[:, :TOK_DEV] + jnp.roll(value_grad[:, TOK_DEV:], -1, axis=0)
            head_queries.append(query_grad.astype(jnp.bfloat16))
            grad_pair = jnp.stack([key_total, value_total], axis=2).astype(jnp.bfloat16)
            head_kv.append(grad_pair)
            value_flat = grad_pair[:, :, 1].reshape(SEQ, HD)
            proj_total = proj_total.at[head].add(jnp.dot(features.T, value_flat, preferred_element_type=jnp.float32))
        query_parts.append(jnp.stack(head_queries, axis=2).reshape(SEQ, HEADS * HD))
        kv_parts.append(jnp.stack(head_kv, axis=2).reshape(SEQ, KVH * 2 * HD))
    return jnp.stack(query_parts), jnp.stack(kv_parts), proj_total
```

```python
import jax
import jax.numpy as jnp
from jax import lax
from jax.sharding import PartitionSpec as P

HD = 128


def shifted(block, axis, distance):
    devices = range(lax.axis_size(axis))
    route = [((i - distance) % len(devices), i) for i in devices]
    return lax.ppermute(block, axis, route)


def token_positions(device, tok_rows, cycle_size):
    half_len = tok_rows // 2
    offsets = jnp.arange(tok_rows, dtype=jnp.int32)
    early = offsets < half_len
    later = (2 * cycle_size - 1 - device) * half_len + offsets - half_len
    return jnp.where(early, device * half_len + offsets, later)


def per_device(queries, keys_values, outputs, grad_out, logsumexp, doc_ids, inputs):
    tok_rows = queries.shape[1]
    head_dim = HD
    group_size = queries.shape[2] // head_dim
    cycle_size = lax.axis_size("context")
    cycle_index = lax.axis_index("context")
    prev_index = (cycle_index - 1 + cycle_size) % cycle_size
    scaling = head_dim ** (-0.5)
    visiting = shifted(keys_values, "context", 1)
    key_value_rows = jnp.concatenate([keys_values[0], visiting[0]], axis=0)
    key_rows = key_value_rows[:, :head_dim]
    value_rows = key_value_rows[:, head_dim:]
    seq_docs = doc_ids[0]
    own_docs = lax.dynamic_slice_in_dim(seq_docs, cycle_index * tok_rows, tok_rows)
    prev_docs = lax.dynamic_slice_in_dim(seq_docs, prev_index * tok_rows, tok_rows)
    query_pos = token_positions(cycle_index, tok_rows, cycle_size)
    key_pos = jnp.concatenate([query_pos, token_positions(prev_index, tok_rows, cycle_size)])
    key_docs = jnp.concatenate([own_docs, prev_docs])
    visible = (key_pos[None, :] <= query_pos[:, None]) & (key_docs[None, :] == own_docs[:, None])
    query_block = queries[0].reshape(tok_rows, group_size, head_dim)
    grad_block = grad_out[0].reshape(tok_rows, group_size, head_dim)
    output_block = outputs[0].reshape(tok_rows, group_size, head_dim)
    lse_block = logsumexp[0]
    scores = jnp.einsum("qgd,kd->gqk", query_block, key_rows, preferred_element_type=jnp.float32)
    attn_prob = jnp.where(
        visible[None], jnp.exp(scores * scaling - lse_block[:, :, None]), jnp.float32(0.0)
    )
    row_delta = jnp.sum(grad_block.astype(jnp.float32) * output_block.astype(jnp.float32), axis=2).T
    grad_prob = jnp.einsum(
        "qgd,kd->gqk", grad_block, value_rows, preferred_element_type=jnp.float32
    )
    grad_score = attn_prob * (grad_prob - row_delta[:, :, None])
    prob_half = attn_prob.astype(jnp.bfloat16)
    score_half = grad_score.astype(jnp.bfloat16)
    value_grad = jnp.einsum(
        "gqk,qgd->kd", prob_half, grad_block, preferred_element_type=jnp.float32
    )
    key_grad = scaling * jnp.einsum(
        "gqk,qgd->kd", score_half, query_block, preferred_element_type=jnp.float32
    )
    query_grad = scaling * jnp.einsum(
        "gqk,kd->qgd", score_half, key_rows, preferred_element_type=jnp.float32
    )
    local_grad = jnp.concatenate([key_grad, value_grad], axis=1)
    returned = shifted(local_grad[tok_rows:], "context", -1)
    grad_kv = (local_grad[:tok_rows] + returned).astype(jnp.bfloat16)
    value_half = grad_kv[:, head_dim:]
    features = inputs[0]
    dp_size = lax.axis_size("dp")
    share_rows = features.shape[1] // (cycle_size * dp_size)
    partial = lax.dot_general(
        features, value_half, (((0,), (0,)), ((), ())), preferred_element_type=jnp.float32
    ).astype(jnp.bfloat16)
    shares = lax.all_to_all(partial, ("context", "dp"), 0, 0, tiled=True)
    proj_grad = jnp.sum(
        shares.reshape(cycle_size * dp_size, share_rows, head_dim).astype(jnp.float32), axis=0
    )
    grad_queries = query_grad.astype(jnp.bfloat16).reshape(1, tok_rows, group_size * head_dim)
    return (
        grad_queries,
        grad_kv.reshape(1, tok_rows, 2 * head_dim),
        proj_grad.reshape(1, share_rows, head_dim),
    )


def solution(mesh):
    in_specs = (
        P("dp", "context", "tensor"),
        P("dp", "context", "tensor"),
        P("dp", "context", "tensor"),
        P("dp", "context", "tensor"),
        P("dp", "tensor", "context"),
        P("dp", None),
        P("dp", "context", None),
    )
    out_specs = (
        P("dp", "context", "tensor"),
        P("dp", "context", "tensor"),
        P("tensor", ("context", "dp"), None),
    )
    return jax.shard_map(
        per_device, mesh=mesh, in_specs=in_specs, out_specs=out_specs, check_vma=False
    )
```

```python
import functools
import math

import jax
import jax.numpy as jnp
from jax import lax
from jax.experimental import pallas as pl
from jax.experimental.pallas import tpu as pltpu
from jax.sharding import PartitionSpec as P

HD = 128
HALF = 128
F32 = jnp.float32
BF16 = jnp.bfloat16
LOG2E = 1.0 / math.log(2.0)
SCALING = HD ** -0.5
NT = (((1,), (1,)), ((), ()))
NN = (((1,), (0,)), ((), ()))
TN = (((0,), (0,)), ((), ()))


def dot(a, b, dims):
    return lax.dot_general(a, b, dims, preferred_element_type=F32)


def shifted(block, axis, distance):
    devices = range(lax.axis_size(axis))
    route = [((i - distance) % len(devices), i) for i in devices]
    return lax.ppermute(block, axis, route)


def down(row):
    return jnp.transpose(jnp.broadcast_to(row, (HALF, HALF)))


def halves(docs_ref, stretch):
    row = docs_ref[stretch].astype(F32)
    return row[:, :HALF], row[:, HALF:]


def own_masks(docs_ref):
    early, late = halves(docs_ref, 0)
    early_down, late_down = down(early), down(late)
    causal = lax.broadcasted_iota(jnp.int32, (HALF, HALF), 0) <= lax.broadcasted_iota(
        jnp.int32, (HALF, HALF), 1
    )
    return causal & (early_down == early), early_down == late, causal & (late_down == late)


def prev_masks(docs_ref, is_first):
    early, late = halves(docs_ref, 0)
    key_early, key_late = halves(docs_ref, 1)
    key_other = jnp.where(is_first, key_late, key_early)
    return down(key_early) == late, down(key_other) == jnp.where(is_first, late, early)


def other_offset():
    return pl.multiple_of(jnp.where(lax.axis_index("context") == 0, HALF, 0), HALF)


def prob_of(scores, lse_row, visible):
    return jnp.where(
        visible, jnp.exp2(scores * (SCALING * LOG2E) - lse_row * LOG2E), jnp.float32(0.0)
    )


def swap_order(x_size, z_size):
    odd = lax.rem(lax.axis_index("tensor"), 2)
    return lambda x, z: jnp.where(odd == 1, x * z_size + z, z * x_size + x)


def own_values(
    heads, cycle_size, x_size, z_size, q_hbm, kv_hbm, lse_hbm, do_hbm, docs_hbm, x_hbm,
    dv_ref, xt_ref, q_ref, kv_ref, lse_ref, do_ref, docs_ref, x_ref, sems,
):
    me = lax.axis_index("context")
    prev = lax.rem(me + cycle_size - 1, cycle_size)
    rows = 2 * HALF

    def docs_of(stretch):
        return docs_hbm.at[:, pl.ds(pl.multiple_of(stretch * rows, rows), rows)]

    pairs = [
        (q_hbm, q_ref), (kv_hbm, kv_ref), (lse_hbm, lse_ref), (do_hbm, do_ref),
        (docs_of(me), docs_ref.at[0]), (docs_of(prev), docs_ref.at[1]), (x_hbm, x_ref),
    ]
    copies = [
        pltpu.make_async_copy(source, target, sems.at[i])
        for i, (source, target) in enumerate(pairs)
    ]
    for copy in copies:
        copy.start()
    for copy in copies[:-1]:
        copy.wait()
    see_ee, see_el, see_ll = own_masks(docs_ref)
    key_early, key_late = kv_ref[0, :HALF, :HD], kv_ref[0, HALF:, :HD]
    early = jnp.zeros((HALF, HD), F32)
    late = jnp.zeros((HALF, HD), F32)
    for h in range(heads):
        cols = slice(h * HD, (h + 1) * HD)
        scores_early = dot(key_early, q_ref[0, :, cols], NT)
        scores_late = dot(key_late, q_ref[0, HALF:, cols], NT)
        lse_e, lse_l = lse_ref[0, h : h + 1, :HALF], lse_ref[0, h : h + 1, HALF:]
        prob_early = jnp.concatenate(
            [
                prob_of(scores_early[:, :HALF], lse_e, see_ee).astype(BF16),
                prob_of(scores_early[:, HALF:], lse_l, see_el).astype(BF16),
            ],
            axis=1,
        )
        prob_late = prob_of(scores_late, lse_l, see_ll).astype(BF16)
        early = early + dot(prob_early, do_ref[0, :, cols], NN)
        late = late + dot(prob_late, do_ref[0, HALF:, cols], NN)
    dv_ref[:HALF] = early
    dv_ref[HALF:] = late
    copies[-1].wait()
    place = swap_order(x_size, z_size)
    chunk = x_ref.shape[2] // (x_size * z_size)
    for x in range(x_size):
        wide = chunk * z_size
        turned = jnp.transpose(x_ref[0, :, x * wide : (x + 1) * wide])
        for z in range(z_size):
            start = pl.multiple_of(place(x, z) * chunk, chunk)
            xt_ref[pl.ds(start, chunk)] = turned[z * chunk : (z + 1) * chunk]


def prev_values(heads, q_ref, kv_ref, lse_ref, do_ref, docs_ref, dv_ref):
    offset = other_offset()
    see_late, see_other = prev_masks(docs_ref, offset > 0)
    key_early, key_other = kv_ref[0, :HALF, :HD], kv_ref[0, pl.ds(offset, HALF), :HD]
    first = jnp.zeros((HALF, HD), F32)
    other = jnp.zeros((HALF, HD), F32)
    for h in range(heads):
        cols = slice(h * HD, (h + 1) * HD)
        scores_late = dot(key_early, q_ref[0, HALF:, cols], NT)
        scores_other = dot(key_other, q_ref[0, pl.ds(offset, HALF), cols], NT)
        lse_l = lse_ref[0, h : h + 1, HALF:]
        lse_o = lse_ref[0, h : h + 1, pl.ds(offset, HALF)]
        prob_late = prob_of(scores_late, lse_l, see_late).astype(BF16)
        prob_other = prob_of(scores_other, lse_o, see_other).astype(BF16)
        first = first + dot(prob_late, do_ref[0, HALF:, cols], NN)
        other = other + dot(prob_other, do_ref[0, pl.ds(offset, HALF), cols], NN)
    is_first = offset > 0
    dv_ref[:HALF] = jnp.where(is_first, first, first + other).astype(BF16)
    dv_ref[HALF:] = jnp.where(is_first, other, jnp.zeros_like(other)).astype(BF16)


def project(xt_ref, own_ref, back_ref, part_hbm, dv_ref, part_ref, sems):
    value_half = (own_ref[...] + back_ref[...].astype(F32)).astype(BF16)
    dv_ref[...] = value_half
    pieces = sems.shape[0]
    rows = part_ref.shape[0] // pieces
    copies = []
    for i in range(pieces):
        piece = slice(i * rows, (i + 1) * rows)
        part_ref[piece] = dot(xt_ref[piece], value_half, NN).astype(BF16)
        copies.append(
            pltpu.make_async_copy(part_ref.at[piece], part_hbm.at[piece], sems.at[i])
        )
        copies[-1].start()
    for copy in copies:
        copy.wait()


def rest(
    heads, q_ref, kv_ref, prev_ref, lse_ref, do_ref, out_ref, docs_ref, after_ref,
    dq_ref, dk_ref, dk_prev_ref, acc_ref,
):
    offset = other_offset()
    see_ee, see_el, see_ll = own_masks(docs_ref)
    see_pl, see_other = prev_masks(docs_ref, offset > 0)
    key_e, key_l = kv_ref[0, :HALF, :HD], kv_ref[0, HALF:, :HD]
    val_e, val_l = kv_ref[0, :HALF, HD:], kv_ref[0, HALF:, HD:]
    key_p, val_p = prev_ref[0, :HALF, :HD], prev_ref[0, :HALF, HD:]
    key_o, val_o = prev_ref[0, pl.ds(offset, HALF), :HD], prev_ref[0, pl.ds(offset, HALF), HD:]
    lane = lax.broadcasted_iota(jnp.int32, (2 * HALF, HD), 1)
    deltas = jnp.zeros((2 * HALF, HD), F32)
    for h in range(heads):
        cols = slice(h * HD, (h + 1) * HD)
        row_sum = jnp.sum(
            do_ref[0, :, cols].astype(F32) * out_ref[0, :, cols].astype(F32), axis=1, keepdims=True
        )
        deltas = jnp.where(lane == h, row_sum, deltas)
    deltas = jnp.transpose(deltas)
    other_deltas = jnp.where(offset > 0, deltas[:, HALF:], deltas[:, :HALF])
    zero = jnp.zeros((HALF, HD), F32)
    dk_e, dk_l, dk_p, dk_o = zero, zero, zero, zero
    keys_late = jnp.concatenate([key_e, key_l, key_p], axis=0)
    for h in range(heads):
        cols = slice(h * HD, (h + 1) * HD)
        q_h, do_h = q_ref[0, :, cols], do_ref[0, :, cols]
        q_l, do_l = q_ref[0, HALF:, cols], do_ref[0, HALF:, cols]
        q_o, do_o = q_ref[0, pl.ds(offset, HALF), cols], do_ref[0, pl.ds(offset, HALF), cols]
        lse_e, lse_l = lse_ref[0, h : h + 1, :HALF], lse_ref[0, h : h + 1, HALF:]
        lse_o = lse_ref[0, h : h + 1, pl.ds(offset, HALF)]
        delta_e, delta_l = deltas[h : h + 1, :HALF], deltas[h : h + 1, HALF:]
        delta_o = other_deltas[h : h + 1]

        s_e, g_e = dot(key_e, q_h, NT), dot(val_e, do_h, NT)
        ds_ee = (prob_of(s_e[:, :HALF], lse_e, see_ee) * (g_e[:, :HALF] - delta_e)).astype(BF16)
        ds_el = (prob_of(s_e[:, HALF:], lse_l, see_el) * (g_e[:, HALF:] - delta_l)).astype(BF16)
        ds_ll = (
            prob_of(dot(key_l, q_l, NT), lse_l, see_ll) * (dot(val_l, do_l, NT) - delta_l)
        ).astype(BF16)
        ds_pl = (
            prob_of(dot(key_p, q_l, NT), lse_l, see_pl) * (dot(val_p, do_l, NT) - delta_l)
        ).astype(BF16)
        ds_o = (
            prob_of(dot(key_o, q_o, NT), lse_o, see_other) * (dot(val_o, do_o, NT) - delta_o)
        ).astype(BF16)
        dk_e = dk_e + dot(jnp.concatenate([ds_ee, ds_el], axis=1), q_h, NN)
        dk_l = dk_l + dot(ds_ll, q_l, NN)
        dk_p = dk_p + dot(ds_pl, q_l, NN)
        dk_o = dk_o + dot(ds_o, q_o, NN)
        acc_ref[:HALF] = dot(ds_ee, key_e, TN)
        acc_ref[HALF:] = dot(jnp.concatenate([ds_el, ds_ll, ds_pl], axis=0), keys_late, TN)
        acc_ref[pl.ds(offset, HALF)] += dot(ds_o, key_o, TN)
        dq_ref[0, :, cols] = (SCALING * acc_ref[...]).astype(BF16)
    is_first = offset > 0
    dk_ref[:HALF] = SCALING * dk_e
    dk_ref[HALF:] = SCALING * dk_l
    dk_prev_ref[:HALF] = (SCALING * jnp.where(is_first, dk_p, dk_p + dk_o)).astype(BF16)
    dk_prev_ref[HALF:] = (SCALING * jnp.where(is_first, dk_o, zero)).astype(BF16)


def call(body, outs, places, flops, moved, name, scratch=(), out_places=None):
    return pl.pallas_call(
        body,
        out_shape=outs,
        in_specs=[pl.BlockSpec(memory_space=place) for place in places],
        out_specs=[
            pl.BlockSpec(memory_space=place) for place in out_places or [pltpu.VMEM] * len(outs)
        ],
        scratch_shapes=list(scratch),
        compiler_params=pltpu.CompilerParams(vmem_limit_bytes=24 * 1024 * 1024),
        cost_estimate=pl.CostEstimate(flops=flops, bytes_accessed=moved, transcendentals=0),
        name=name,
    )


def sum_over(shares, rows):
    return jnp.sum(shares.reshape(-1, rows, HD).astype(F32), axis=0)


def scattered(partial, x_size, z_size):
    axes = ("context", "dp", "tensor")
    n_dp, n_tensor = lax.axis_size("dp"), lax.axis_size("tensor")

    def index(x, z, d, t):
        return ((x * z_size + z) * n_dp + d) * n_tensor + t

    first, second = [], []
    for t in range(n_tensor):
        odd = t % 2 == 1
        for fixed in range(x_size if not odd else z_size):
            for d in range(n_dp):
                first.append(
                    [index(j, fixed, d, t) for j in range(x_size)] if odd
                    else [index(fixed, j, d, t) for j in range(z_size)]
                )
        for fixed in range(z_size if not odd else x_size):
            second.append(
                [index(fixed, j, d, t) for j in range(z_size) for d in range(n_dp)] if odd
                else [index(j, fixed, d, t) for j in range(x_size) for d in range(n_dp)]
            )
    shares = lax.all_to_all(partial, axes, 0, 0, axis_index_groups=first, tiled=True)
    sums = sum_over(shares, partial.shape[0] // z_size).astype(BF16)
    shares = lax.all_to_all(sums, axes, 0, 0, axis_index_groups=second, tiled=True)
    return sum_over(shares, sums.shape[0] // (x_size * n_dp))


def per_device(queries, keys_values, outputs, grad_out, logsumexp, doc_ids, inputs):
    tok_rows = queries.shape[1]
    heads = queries.shape[2] // HD
    features = inputs.shape[2]
    cycle_size = lax.axis_size("context")
    x_size = z_size = math.isqrt(cycle_size)
    shape = jax.ShapeDtypeStruct
    hbm, vmem = pltpu.HBM, pltpu.VMEM

    queries, grad_out, logsumexp, doc_ids, inputs, outputs = (
        pltpu.with_memory_space_constraint(a, pltpu.HBM)
        for a in (queries, grad_out, logsumexp, doc_ids, inputs, outputs)
    )
    visiting = shifted(keys_values, "context", 1)
    dv_own, turned, q_near, kv_near, lse_near, do_near, docs_near = call(
        functools.partial(own_values, heads, cycle_size, x_size, z_size),
        [
            shape((tok_rows, HD), F32), shape((features, tok_rows), BF16),
            shape(queries.shape, BF16), shape(keys_values.shape, BF16),
            shape(logsumexp.shape, F32), shape(grad_out.shape, BF16),
            shape((2, 1, tok_rows), jnp.int32),
        ],
        [hbm] * 6, 400_000_000, 6_000_000, "own_values",
        scratch=[pltpu.VMEM(inputs.shape, BF16), pltpu.SemaphoreType.DMA((7,))],
    )(queries, keys_values, logsumexp, grad_out, doc_ids, inputs)
    (dv_prev,) = call(
        functools.partial(prev_values, heads), [shape((tok_rows, HD), BF16)],
        [vmem] * 5, 300_000_000, 1_200_000, "prev_values",
    )(q_near, visiting, lse_near, do_near, docs_near)
    dv_back = shifted(dv_prev, "context", -1)
    partial, dv_half = call(
        project, [shape((features, HD), BF16), shape((tok_rows, HD), BF16)],
        [vmem] * 3, 300_000_000, 3_000_000, "project",
        scratch=[pltpu.VMEM((features, HD), BF16), pltpu.SemaphoreType.DMA((8,))], out_places=[hbm, vmem],
    )(turned, dv_own, dv_back)
    proj_grad = scattered(partial, x_size, z_size)
    dq, dk_own, dk_prev = call(
        functools.partial(rest, heads),
        [
            shape(queries.shape, BF16), shape((tok_rows, HD), F32), shape((tok_rows, HD), BF16),
        ],
        [vmem] * 7 + [pl.ANY], 2_000_000_000, 3_000_000, "rest",
        scratch=[pltpu.VMEM((tok_rows, HD), F32)],
    )(q_near, kv_near, visiting, lse_near, do_near, outputs, docs_near, dv_half)
    dk_back = shifted(dk_prev, "context", -1)
    dk_half = (dk_own + dk_back.astype(F32)).astype(BF16)
    grad_kv = jnp.concatenate([dk_half, dv_half], axis=1)
    return dq, grad_kv[None], proj_grad[None]


def solution(mesh):
    in_specs = (
        P("dp", "context", "tensor"),
        P("dp", "context", "tensor"),
        P("dp", "context", "tensor"),
        P("dp", "context", "tensor"),
        P("dp", "tensor", "context"),
        P("dp", None),
        P("dp", "context", None),
    )
    out_specs = (
        P("dp", "context", "tensor"),
        P("dp", "context", "tensor"),
        P("tensor", ("context", "dp"), None),
    )
    return jax.shard_map(
        per_device, mesh=mesh, in_specs=in_specs, out_specs=out_specs, check_vma=False
    )
```

```python
import functools
import math

import jax
import jax.numpy as jnp
from jax import lax
from jax.experimental import pallas as pl
from jax.experimental.pallas import tpu as pltpu
from jax.sharding import PartitionSpec as P

HD = 128
HALF = 128
F32 = jnp.float32
BF16 = jnp.bfloat16
LOG2E = 1.0 / math.log(2.0)
SCALING = HD ** -0.5
NT = (((1,), (1,)), ((), ()))
NN = (((1,), (0,)), ((), ()))
TN = (((0,), (0,)), ((), ()))


def dot(a, b, dims):
    return lax.dot_general(a, b, dims, preferred_element_type=F32)


def shifted(block, axis, distance):
    devices = range(lax.axis_size(axis))
    route = [((i - distance) % len(devices), i) for i in devices]
    return lax.ppermute(block, axis, route)


def down(row):
    return jnp.transpose(jnp.broadcast_to(row, (HALF, HALF)))


def halves(docs_ref, stretch):
    row = docs_ref[stretch].astype(F32)
    return row[:, :HALF], row[:, HALF:]


def own_masks(docs_ref):
    early, late = halves(docs_ref, 0)
    early_down, late_down = down(early), down(late)
    causal = lax.broadcasted_iota(jnp.int32, (HALF, HALF), 0) <= lax.broadcasted_iota(
        jnp.int32, (HALF, HALF), 1
    )
    return causal & (early_down == early), early_down == late, causal & (late_down == late)


def prev_masks(docs_ref, is_first):
    early, late = halves(docs_ref, 0)
    key_early, key_late = halves(docs_ref, 1)
    key_other = jnp.where(is_first, key_late, key_early)
    return down(key_early) == late, down(key_other) == jnp.where(is_first, late, early)


def other_offset():
    return pl.multiple_of(jnp.where(lax.axis_index("context") == 0, HALF, 0), HALF)


def prob_of(scores, lse_row, visible):
    return jnp.where(
        visible, jnp.exp2(scores * (SCALING * LOG2E) - lse_row * LOG2E), jnp.float32(0.0)
    )


def swap_order(x_size, z_size):
    odd = lax.rem(lax.axis_index("tensor"), 2)
    return lambda x, z: jnp.where(odd == 0, x * z_size + z, z * x_size + x)


def own_values(
    heads, cycle_size, x_size, z_size, q_hbm, kv_hbm, lse_hbm, do_hbm, docs_hbm, x_hbm,
    dv_ref, xt_ref, q_ref, kv_ref, lse_ref, do_ref, docs_ref, x_ref, sems,
):
    me = lax.axis_index("context")
    prev = lax.rem(me + cycle_size - 1, cycle_size)
    rows = 2 * HALF

    def docs_of(stretch):
        return docs_hbm.at[:, pl.ds(pl.multiple_of(stretch * rows, rows), rows)]

    pairs = [
        (q_hbm, q_ref), (kv_hbm, kv_ref), (lse_hbm, lse_ref), (do_hbm, do_ref),
        (docs_of(me), docs_ref.at[0]), (docs_of(prev), docs_ref.at[1]), (x_hbm, x_ref),
    ]
    copies = [
        pltpu.make_async_copy(source, target, sems.at[i])
        for i, (source, target) in enumerate(pairs)
    ]
    for copy in copies:
        copy.start()
    for copy in copies[:-1]:
        copy.wait()
    see_ee, see_el, see_ll = own_masks(docs_ref)
    key_early, key_late = kv_ref[0, :HALF, :HD], kv_ref[0, HALF:, :HD]
    early = jnp.zeros((HALF, HD), F32)
    late = jnp.zeros((HALF, HD), F32)
    for h in range(heads):
        cols = slice(h * HD, (h + 1) * HD)
        scores_early = dot(key_early, q_ref[0, :, cols], NT)
        scores_late = dot(key_late, q_ref[0, HALF:, cols], NT)
        lse_e, lse_l = lse_ref[0, h : h + 1, :HALF], lse_ref[0, h : h + 1, HALF:]
        prob_early = jnp.concatenate(
            [
                prob_of(scores_early[:, :HALF], lse_e, see_ee).astype(BF16),
                prob_of(scores_early[:, HALF:], lse_l, see_el).astype(BF16),
            ],
            axis=1,
        )
        prob_late = prob_of(scores_late, lse_l, see_ll).astype(BF16)
        early = early + dot(prob_early, do_ref[0, :, cols], NN)
        late = late + dot(prob_late, do_ref[0, HALF:, cols], NN)
    dv_ref[:HALF] = early
    dv_ref[HALF:] = late
    copies[-1].wait()
    place = swap_order(x_size, z_size)
    chunk = x_ref.shape[2] // (x_size * z_size)
    for x in range(x_size):
        wide = chunk * z_size
        turned = jnp.transpose(x_ref[0, :, x * wide : (x + 1) * wide])
        for z in range(z_size):
            start = pl.multiple_of(place(x, z) * chunk, chunk)
            xt_ref[pl.ds(start, chunk)] = turned[z * chunk : (z + 1) * chunk]


def prev_values(heads, q_ref, kv_ref, lse_ref, do_ref, docs_ref, dv_ref):
    offset = other_offset()
    see_late, see_other = prev_masks(docs_ref, offset > 0)
    key_early, key_other = kv_ref[0, :HALF, :HD], kv_ref[0, pl.ds(offset, HALF), :HD]
    first = jnp.zeros((HALF, HD), F32)
    other = jnp.zeros((HALF, HD), F32)
    for h in range(heads):
        cols = slice(h * HD, (h + 1) * HD)
        scores_late = dot(key_early, q_ref[0, HALF:, cols], NT)
        scores_other = dot(key_other, q_ref[0, pl.ds(offset, HALF), cols], NT)
        lse_l = lse_ref[0, h : h + 1, HALF:]
        lse_o = lse_ref[0, h : h + 1, pl.ds(offset, HALF)]
        prob_late = prob_of(scores_late, lse_l, see_late).astype(BF16)
        prob_other = prob_of(scores_other, lse_o, see_other).astype(BF16)
        first = first + dot(prob_late, do_ref[0, HALF:, cols], NN)
        other = other + dot(prob_other, do_ref[0, pl.ds(offset, HALF), cols], NN)
    is_first = offset > 0
    dv_ref[:HALF] = jnp.where(is_first, first, first + other).astype(BF16)
    dv_ref[HALF:] = jnp.where(is_first, other, jnp.zeros_like(other)).astype(BF16)


def project(xt_ref, own_ref, back_ref, part_hbm, dv_ref, part_ref, sems):
    value_half = (own_ref[...] + back_ref[...].astype(F32)).astype(BF16)
    dv_ref[...] = value_half
    pieces = sems.shape[0]
    rows = part_ref.shape[0] // pieces
    copies = []
    for i in range(pieces):
        piece = slice(i * rows, (i + 1) * rows)
        part_ref[piece] = dot(xt_ref[piece], value_half, NN).astype(BF16)
        copies.append(
            pltpu.make_async_copy(part_ref.at[piece], part_hbm.at[piece], sems.at[i])
        )
        copies[-1].start()
    for copy in copies:
        copy.wait()


def add_up(shares_ref, sum_ref):
    total = shares_ref[0].astype(F32)
    for i in range(1, shares_ref.shape[0]):
        total = total + shares_ref[i].astype(F32)
    sum_ref[...] = total.astype(BF16)


def rest(
    heads, q_ref, kv_ref, prev_ref, lse_ref, do_ref, out_ref, docs_ref, after_ref,
    dq_ref, dk_ref, dk_prev_ref, acc_ref,
):
    offset = other_offset()
    see_ee, see_el, see_ll = own_masks(docs_ref)
    see_pl, see_other = prev_masks(docs_ref, offset > 0)
    key_e, key_l = kv_ref[0, :HALF, :HD], kv_ref[0, HALF:, :HD]
    val_e, val_l = kv_ref[0, :HALF, HD:], kv_ref[0, HALF:, HD:]
    key_p, val_p = prev_ref[0, :HALF, :HD], prev_ref[0, :HALF, HD:]
    key_o, val_o = prev_ref[0, pl.ds(offset, HALF), :HD], prev_ref[0, pl.ds(offset, HALF), HD:]
    lane = lax.broadcasted_iota(jnp.int32, (2 * HALF, HD), 1)
    deltas = jnp.zeros((2 * HALF, HD), F32)
    for h in range(heads):
        cols = slice(h * HD, (h + 1) * HD)
        row_sum = jnp.sum(
            do_ref[0, :, cols].astype(F32) * out_ref[0, :, cols].astype(F32), axis=1, keepdims=True
        )
        deltas = jnp.where(lane == h, row_sum, deltas)
    deltas = jnp.transpose(deltas)
    other_deltas = jnp.where(offset > 0, deltas[:, HALF:], deltas[:, :HALF])
    zero = jnp.zeros((HALF, HD), F32)
    dk_e, dk_l, dk_p, dk_o = zero, zero, zero, zero
    keys_late = jnp.concatenate([key_e, key_l, key_p], axis=0)
    for h in range(heads):
        cols = slice(h * HD, (h + 1) * HD)
        q_h, do_h = q_ref[0, :, cols], do_ref[0, :, cols]
        q_l, do_l = q_ref[0, HALF:, cols], do_ref[0, HALF:, cols]
        q_o, do_o = q_ref[0, pl.ds(offset, HALF), cols], do_ref[0, pl.ds(offset, HALF), cols]
        lse_e, lse_l = lse_ref[0, h : h + 1, :HALF], lse_ref[0, h : h + 1, HALF:]
        lse_o = lse_ref[0, h : h + 1, pl.ds(offset, HALF)]
        delta_e, delta_l = deltas[h : h + 1, :HALF], deltas[h : h + 1, HALF:]
        delta_o = other_deltas[h : h + 1]

        s_e, g_e = dot(key_e, q_h, NT), dot(val_e, do_h, NT)
        ds_ee = (prob_of(s_e[:, :HALF], lse_e, see_ee) * (g_e[:, :HALF] - delta_e)).astype(BF16)
        ds_el = (prob_of(s_e[:, HALF:], lse_l, see_el) * (g_e[:, HALF:] - delta_l)).astype(BF16)
        ds_ll = (
            prob_of(dot(key_l, q_l, NT), lse_l, see_ll) * (dot(val_l, do_l, NT) - delta_l)
        ).astype(BF16)
        ds_pl = (
            prob_of(dot(key_p, q_l, NT), lse_l, see_pl) * (dot(val_p, do_l, NT) - delta_l)
        ).astype(BF16)
        ds_o = (
            prob_of(dot(key_o, q_o, NT), lse_o, see_other) * (dot(val_o, do_o, NT) - delta_o)
        ).astype(BF16)
        dk_e = dk_e + dot(jnp.concatenate([ds_ee, ds_el], axis=1), q_h, NN)
        dk_l = dk_l + dot(ds_ll, q_l, NN)
        dk_p = dk_p + dot(ds_pl, q_l, NN)
        dk_o = dk_o + dot(ds_o, q_o, NN)
        acc_ref[:HALF] = dot(ds_ee, key_e, TN)
        acc_ref[HALF:] = dot(jnp.concatenate([ds_el, ds_ll, ds_pl], axis=0), keys_late, TN)
        acc_ref[pl.ds(offset, HALF)] += dot(ds_o, key_o, TN)
        dq_ref[0, :, cols] = (SCALING * acc_ref[...]).astype(BF16)
    is_first = offset > 0
    dk_ref[:HALF] = SCALING * dk_e
    dk_ref[HALF:] = SCALING * dk_l
    dk_prev_ref[:HALF] = (SCALING * jnp.where(is_first, dk_p, dk_p + dk_o)).astype(BF16)
    dk_prev_ref[HALF:] = (SCALING * jnp.where(is_first, dk_o, zero)).astype(BF16)


def call(body, outs, places, flops, moved, name, scratch=(), out_places=None):
    return pl.pallas_call(
        body,
        out_shape=outs,
        in_specs=[pl.BlockSpec(memory_space=place) for place in places],
        out_specs=[
            pl.BlockSpec(memory_space=place) for place in out_places or [pltpu.VMEM] * len(outs)
        ],
        scratch_shapes=list(scratch),
        compiler_params=pltpu.CompilerParams(vmem_limit_bytes=24 * 1024 * 1024),
        cost_estimate=pl.CostEstimate(flops=flops, bytes_accessed=moved, transcendentals=0),
        name=name,
    )


def sum_over(shares, rows):
    return jnp.sum(shares.reshape(-1, rows, HD).astype(F32), axis=0)


def scattered(partial, x_size, z_size):
    axes = ("context", "dp", "tensor")
    n_dp, n_tensor = lax.axis_size("dp"), lax.axis_size("tensor")

    def index(x, z, d, t):
        return ((x * z_size + z) * n_dp + d) * n_tensor + t

    first, second = [], []
    for t in range(n_tensor):
        x_first = t % 2 == 0
        for fixed in range(x_size if not x_first else z_size):
            for d in range(n_dp):
                first.append(
                    [index(j, fixed, d, t) for j in range(x_size)] if x_first
                    else [index(fixed, j, d, t) for j in range(z_size)]
                )
        for fixed in range(z_size if not x_first else x_size):
            second.append(
                [index(fixed, j, d, t) for j in range(z_size) for d in range(n_dp)] if x_first
                else [index(j, fixed, d, t) for j in range(x_size) for d in range(n_dp)]
            )
    shares = lax.all_to_all(partial, axes, 0, 0, axis_index_groups=first, tiled=True)
    rows = partial.shape[0] // z_size
    (sums,) = call(
        add_up, [jax.ShapeDtypeStruct((rows, HD), BF16)], [pltpu.VMEM], 2_000_000, 1_200_000,
        "add_up",
    )(shares.reshape(z_size, rows, HD))
    shares = lax.all_to_all(sums, axes, 0, 0, axis_index_groups=second, tiled=True)
    return sum_over(shares, sums.shape[0] // (x_size * n_dp))


def per_device(queries, keys_values, outputs, grad_out, logsumexp, doc_ids, inputs):
    tok_rows = queries.shape[1]
    heads = queries.shape[2] // HD
    features = inputs.shape[2]
    cycle_size = lax.axis_size("context")
    x_size = z_size = math.isqrt(cycle_size)
    shape = jax.ShapeDtypeStruct
    hbm, vmem = pltpu.HBM, pltpu.VMEM

    queries, grad_out, logsumexp, doc_ids, inputs, outputs = (
        pltpu.with_memory_space_constraint(a, pltpu.HBM)
        for a in (queries, grad_out, logsumexp, doc_ids, inputs, outputs)
    )
    visiting = shifted(keys_values, "context", 1)
    dv_own, turned, q_near, kv_near, lse_near, do_near, docs_near = call(
        functools.partial(own_values, heads, cycle_size, x_size, z_size),
        [
            shape((tok_rows, HD), F32), shape((features, tok_rows), BF16),
            shape(queries.shape, BF16), shape(keys_values.shape, BF16),
            shape(logsumexp.shape, F32), shape(grad_out.shape, BF16),
            shape((2, 1, tok_rows), jnp.int32),
        ],
        [hbm] * 6, 400_000_000, 6_000_000, "own_values",
        scratch=[pltpu.VMEM(inputs.shape, BF16), pltpu.SemaphoreType.DMA((7,))],
    )(
        queries, pltpu.with_memory_space_constraint(keys_values, pltpu.HBM), logsumexp, grad_out,
        doc_ids, inputs,
    )
    (dv_prev,) = call(
        functools.partial(prev_values, heads), [shape((tok_rows, HD), BF16)],
        [vmem] * 5, 300_000_000, 1_200_000, "prev_values",
    )(q_near, visiting, lse_near, do_near, docs_near)
    dv_back = shifted(dv_prev, "context", -1)
    partial, dv_half = call(
        project, [shape((features, HD), BF16), shape((tok_rows, HD), BF16)],
        [vmem] * 3, 300_000_000, 3_000_000, "project",
        scratch=[pltpu.VMEM((features, HD), BF16), pltpu.SemaphoreType.DMA((8,))], out_places=[hbm, vmem],
    )(turned, dv_own, dv_back)
    proj_grad = scattered(partial, x_size, z_size)
    dq, dk_own, dk_prev = call(
        functools.partial(rest, heads),
        [
            shape(queries.shape, BF16), shape((tok_rows, HD), F32), shape((tok_rows, HD), BF16),
        ],
        [vmem] * 7 + [pl.ANY], 2_000_000_000, 3_000_000, "rest",
        scratch=[pltpu.VMEM((tok_rows, HD), F32)],
    )(q_near, kv_near, visiting, lse_near, do_near, outputs, docs_near, dv_half)
    dk_back = shifted(dk_prev, "context", -1)
    dk_half = (dk_own + dk_back.astype(F32)).astype(BF16)
    grad_kv = jnp.concatenate([dk_half, dv_half], axis=1)
    return dq, grad_kv[None], proj_grad[None]


def solution(mesh):
    in_specs = (
        P("dp", "context", "tensor"),
        P("dp", "context", "tensor"),
        P("dp", "context", "tensor"),
        P("dp", "context", "tensor"),
        P("dp", "tensor", "context"),
        P("dp", None),
        P("dp", "context", None),
    )
    out_specs = (
        P("dp", "context", "tensor"),
        P("dp", "context", "tensor"),
        P("tensor", ("context", "dp"), None),
    )
    return jax.shard_map(
        per_device, mesh=mesh, in_specs=in_specs, out_specs=out_specs, check_vma=False
    )
```

```python
import functools
import math

import jax
import jax.numpy as jnp
from jax import lax
from jax.experimental import pallas as pl
from jax.experimental.pallas import tpu as pltpu
from jax.sharding import PartitionSpec as P

HD = 128
HALF = 128
F32 = jnp.float32
BF16 = jnp.bfloat16
LOG2E = 1.0 / math.log(2.0)
SCALING = HD ** -0.5
NT = (((1,), (1,)), ((), ()))
NN = (((1,), (0,)), ((), ()))
TN = (((0,), (0,)), ((), ()))


def dot(a, b, dims):
    return lax.dot_general(a, b, dims, preferred_element_type=F32)


def shifted(block, axis, distance):
    devices = range(lax.axis_size(axis))
    route = [((i - distance) % len(devices), i) for i in devices]
    return lax.ppermute(block, axis, route)


def down(row):
    return jnp.transpose(jnp.broadcast_to(row, (HALF, HALF)))


def halves(docs_ref, stretch):
    row = docs_ref[stretch].astype(F32)
    return row[:, :HALF], row[:, HALF:]


def own_masks(docs_ref):
    early, late = halves(docs_ref, 0)
    early_down, late_down = down(early), down(late)
    causal = lax.broadcasted_iota(jnp.int32, (HALF, HALF), 0) <= lax.broadcasted_iota(
        jnp.int32, (HALF, HALF), 1
    )
    return causal & (early_down == early), early_down == late, causal & (late_down == late)


def prev_masks(docs_ref, is_first):
    early, late = halves(docs_ref, 0)
    key_early, key_late = halves(docs_ref, 1)
    key_other = jnp.where(is_first, key_late, key_early)
    return down(key_early) == late, down(key_other) == jnp.where(is_first, late, early)


def other_offset():
    return pl.multiple_of(jnp.where(lax.axis_index("context") == 0, HALF, 0), HALF)


def prob_of(scores, lse_row, visible):
    return jnp.where(
        visible, jnp.exp2(scores * (SCALING * LOG2E) - lse_row * LOG2E), jnp.float32(0.0)
    )


def swap_order(x_size, z_size):
    odd = lax.rem(lax.axis_index("tensor"), 2)
    return lambda x, z: jnp.where(odd == 0, x * z_size + z, z * x_size + x)


def own_values(
    heads, cycle_size, x_size, z_size, q_hbm, kv_hbm, lse_hbm, do_hbm, docs_hbm, x_hbm,
    dv_ref, xt_ref, q_ref, kv_ref, lse_ref, do_ref, docs_ref, x_ref, sems,
):
    me = lax.axis_index("context")
    prev = lax.rem(me + cycle_size - 1, cycle_size)
    rows = 2 * HALF

    def docs_of(stretch):
        return docs_hbm.at[:, pl.ds(pl.multiple_of(stretch * rows, rows), rows)]

    pairs = [
        (q_hbm, q_ref), (kv_hbm, kv_ref), (lse_hbm, lse_ref), (do_hbm, do_ref),
        (docs_of(me), docs_ref.at[0]), (docs_of(prev), docs_ref.at[1]), (x_hbm, x_ref),
    ]
    copies = [
        pltpu.make_async_copy(source, target, sems.at[i])
        for i, (source, target) in enumerate(pairs)
    ]
    for copy in copies:
        copy.start()
    for copy in copies[:-1]:
        copy.wait()
    see_ee, see_el, see_ll = own_masks(docs_ref)
    key_early, key_late = kv_ref[0, :HALF, :HD], kv_ref[0, HALF:, :HD]
    early = jnp.zeros((HALF, HD), F32)
    late = jnp.zeros((HALF, HD), F32)
    for h in range(heads):
        cols = slice(h * HD, (h + 1) * HD)
        scores_early = dot(key_early, q_ref[0, :, cols], NT)
        scores_late = dot(key_late, q_ref[0, HALF:, cols], NT)
        lse_e, lse_l = lse_ref[0, h : h + 1, :HALF], lse_ref[0, h : h + 1, HALF:]
        prob_early = jnp.concatenate(
            [
                prob_of(scores_early[:, :HALF], lse_e, see_ee).astype(BF16),
                prob_of(scores_early[:, HALF:], lse_l, see_el).astype(BF16),
            ],
            axis=1,
        )
        prob_late = prob_of(scores_late, lse_l, see_ll).astype(BF16)
        early = early + dot(prob_early, do_ref[0, :, cols], NN)
        late = late + dot(prob_late, do_ref[0, HALF:, cols], NN)
    dv_ref[:HALF] = early
    dv_ref[HALF:] = late
    copies[-1].wait()
    place = swap_order(x_size, z_size)
    chunk = x_ref.shape[2] // (x_size * z_size)
    for x in range(x_size):
        wide = chunk * z_size
        turned = jnp.transpose(x_ref[0, :, x * wide : (x + 1) * wide])
        for z in range(z_size):
            start = pl.multiple_of(place(x, z) * chunk, chunk)
            xt_ref[pl.ds(start, chunk)] = turned[z * chunk : (z + 1) * chunk]


def prev_values(heads, q_ref, kv_ref, lse_ref, do_ref, docs_ref, dv_ref):
    is_first = lax.axis_index("context") == 0
    query_row = docs_ref[0].astype(F32)
    key_early, key_late = halves(docs_ref, 1)
    early_down = down(key_early)

    @pl.when(jnp.logical_not(is_first))
    def _():
        visible = jnp.concatenate([early_down, early_down], axis=1) == query_row
        total = jnp.zeros((HALF, HD), F32)
        for h in range(heads):
            cols = slice(h * HD, (h + 1) * HD)
            scores = dot(kv_ref[0, :HALF, :HD], q_ref[0, :, cols], NT)
            prob = prob_of(scores, lse_ref[0, h : h + 1, :], visible).astype(BF16)
            total = total + dot(prob, do_ref[0, :, cols], NN)
        dv_ref[:HALF] = total.astype(BF16)
        dv_ref[HALF:] = jnp.zeros((HALF, HD), BF16)

    @pl.when(is_first)
    def _():
        visible = jnp.concatenate([early_down, down(key_late)], axis=0) == query_row[:, HALF:]
        total = jnp.zeros((2 * HALF, HD), F32)
        for h in range(heads):
            cols = slice(h * HD, (h + 1) * HD)
            scores = dot(kv_ref[0, :, :HD], q_ref[0, HALF:, cols], NT)
            prob = prob_of(scores, lse_ref[0, h : h + 1, HALF:], visible).astype(BF16)
            total = total + dot(prob, do_ref[0, HALF:, cols], NN)
        dv_ref[...] = total.astype(BF16)


def project(xt_ref, own_ref, back_ref, part_hbm, dv_ref, part_ref, sems):
    value_half = (own_ref[...] + back_ref[...].astype(F32)).astype(BF16)
    dv_ref[...] = value_half
    pieces = sems.shape[0]
    rows = part_ref.shape[0] // pieces
    copies = []
    for i in range(pieces):
        piece = slice(i * rows, (i + 1) * rows)
        part_ref[piece] = dot(xt_ref[piece], value_half, NN).astype(BF16)
        copies.append(
            pltpu.make_async_copy(part_ref.at[piece], part_hbm.at[piece], sems.at[i])
        )
        copies[-1].start()
    for copy in copies:
        copy.wait()


def add_up(shares_ref, sum_ref):
    total = shares_ref[0].astype(F32)
    for i in range(1, shares_ref.shape[0]):
        total = total + shares_ref[i].astype(F32)
    sum_ref[...] = total.astype(BF16)


def rest(
    heads, q_ref, kv_ref, prev_ref, lse_ref, do_ref, out_ref, docs_ref, after_ref,
    dq_ref, dk_ref, dk_prev_ref, acc_ref,
):
    offset = other_offset()
    see_ee, see_el, see_ll = own_masks(docs_ref)
    see_pl, see_other = prev_masks(docs_ref, offset > 0)
    key_e, key_l = kv_ref[0, :HALF, :HD], kv_ref[0, HALF:, :HD]
    val_e, val_l = kv_ref[0, :HALF, HD:], kv_ref[0, HALF:, HD:]
    key_p, val_p = prev_ref[0, :HALF, :HD], prev_ref[0, :HALF, HD:]
    key_o, val_o = prev_ref[0, pl.ds(offset, HALF), :HD], prev_ref[0, pl.ds(offset, HALF), HD:]
    lane = lax.broadcasted_iota(jnp.int32, (2 * HALF, HD), 1)
    deltas = jnp.zeros((2 * HALF, HD), F32)
    for h in range(heads):
        cols = slice(h * HD, (h + 1) * HD)
        row_sum = jnp.sum(
            do_ref[0, :, cols].astype(F32) * out_ref[0, :, cols].astype(F32), axis=1, keepdims=True
        )
        deltas = jnp.where(lane == h, row_sum, deltas)
    deltas = jnp.transpose(deltas)
    other_deltas = jnp.where(offset > 0, deltas[:, HALF:], deltas[:, :HALF])
    zero = jnp.zeros((HALF, HD), F32)
    dk_e, dk_l, dk_p, dk_o = zero, zero, zero, zero
    keys_late = jnp.concatenate([key_e, key_l, key_p], axis=0)
    for h in range(heads):
        cols = slice(h * HD, (h + 1) * HD)
        q_h, do_h = q_ref[0, :, cols], do_ref[0, :, cols]
        q_l, do_l = q_ref[0, HALF:, cols], do_ref[0, HALF:, cols]
        q_o, do_o = q_ref[0, pl.ds(offset, HALF), cols], do_ref[0, pl.ds(offset, HALF), cols]
        lse_e, lse_l = lse_ref[0, h : h + 1, :HALF], lse_ref[0, h : h + 1, HALF:]
        lse_o = lse_ref[0, h : h + 1, pl.ds(offset, HALF)]
        delta_e, delta_l = deltas[h : h + 1, :HALF], deltas[h : h + 1, HALF:]
        delta_o = other_deltas[h : h + 1]

        s_e, g_e = dot(key_e, q_h, NT), dot(val_e, do_h, NT)
        ds_ee = (prob_of(s_e[:, :HALF], lse_e, see_ee) * (g_e[:, :HALF] - delta_e)).astype(BF16)
        ds_el = (prob_of(s_e[:, HALF:], lse_l, see_el) * (g_e[:, HALF:] - delta_l)).astype(BF16)
        ds_ll = (
            prob_of(dot(key_l, q_l, NT), lse_l, see_ll) * (dot(val_l, do_l, NT) - delta_l)
        ).astype(BF16)
        ds_pl = (
            prob_of(dot(key_p, q_l, NT), lse_l, see_pl) * (dot(val_p, do_l, NT) - delta_l)
        ).astype(BF16)
        ds_o = (
            prob_of(dot(key_o, q_o, NT), lse_o, see_other) * (dot(val_o, do_o, NT) - delta_o)
        ).astype(BF16)
        dk_e = dk_e + dot(jnp.concatenate([ds_ee, ds_el], axis=1), q_h, NN)
        dk_l = dk_l + dot(ds_ll, q_l, NN)
        dk_p = dk_p + dot(ds_pl, q_l, NN)
        dk_o = dk_o + dot(ds_o, q_o, NN)
        acc_ref[:HALF] = dot(ds_ee, key_e, TN)
        acc_ref[HALF:] = dot(jnp.concatenate([ds_el, ds_ll, ds_pl], axis=0), keys_late, TN)
        acc_ref[pl.ds(offset, HALF)] += dot(ds_o, key_o, TN)
        dq_ref[0, :, cols] = (SCALING * acc_ref[...]).astype(BF16)
    is_first = offset > 0
    dk_ref[:HALF] = SCALING * dk_e
    dk_ref[HALF:] = SCALING * dk_l
    dk_prev_ref[:HALF] = (SCALING * jnp.where(is_first, dk_p, dk_p + dk_o)).astype(BF16)
    dk_prev_ref[HALF:] = (SCALING * jnp.where(is_first, dk_o, zero)).astype(BF16)


def call(body, outs, places, flops, moved, name, scratch=(), out_places=None):
    return pl.pallas_call(
        body,
        out_shape=outs,
        in_specs=[pl.BlockSpec(memory_space=place) for place in places],
        out_specs=[
            pl.BlockSpec(memory_space=place) for place in out_places or [pltpu.VMEM] * len(outs)
        ],
        scratch_shapes=list(scratch),
        compiler_params=pltpu.CompilerParams(vmem_limit_bytes=24 * 1024 * 1024),
        cost_estimate=pl.CostEstimate(flops=flops, bytes_accessed=moved, transcendentals=0),
        name=name,
    )


def sum_over(shares, rows):
    return jnp.sum(shares.reshape(-1, rows, HD).astype(F32), axis=0)


def scattered(partial, x_size, z_size):
    axes = ("context", "dp", "tensor")
    n_dp, n_tensor = lax.axis_size("dp"), lax.axis_size("tensor")

    def index(x, z, d, t):
        return ((x * z_size + z) * n_dp + d) * n_tensor + t

    first, second = [], []
    for t in range(n_tensor):
        x_first = t % 2 == 0
        for fixed in range(x_size if not x_first else z_size):
            for d in range(n_dp):
                first.append(
                    [index(j, fixed, d, t) for j in range(x_size)] if x_first
                    else [index(fixed, j, d, t) for j in range(z_size)]
                )
        for fixed in range(z_size if not x_first else x_size):
            second.append(
                [index(fixed, j, d, t) for j in range(z_size) for d in range(n_dp)] if x_first
                else [index(j, fixed, d, t) for j in range(x_size) for d in range(n_dp)]
            )
    shares = lax.all_to_all(partial, axes, 0, 0, axis_index_groups=first, tiled=True)
    rows = partial.shape[0] // z_size
    (sums,) = call(
        add_up, [jax.ShapeDtypeStruct((rows, HD), BF16)], [pltpu.VMEM], 2_000_000, 1_200_000,
        "add_up",
    )(shares.reshape(z_size, rows, HD))
    shares = lax.all_to_all(sums, axes, 0, 0, axis_index_groups=second, tiled=True)
    return sum_over(shares, sums.shape[0] // (x_size * n_dp))


def per_device(queries, keys_values, outputs, grad_out, logsumexp, doc_ids, inputs):
    tok_rows = queries.shape[1]
    heads = queries.shape[2] // HD
    features = inputs.shape[2]
    cycle_size = lax.axis_size("context")
    x_size = z_size = math.isqrt(cycle_size)
    shape = jax.ShapeDtypeStruct
    hbm, vmem = pltpu.HBM, pltpu.VMEM

    queries, grad_out, logsumexp, doc_ids, inputs, outputs = (
        pltpu.with_memory_space_constraint(a, pltpu.HBM)
        for a in (queries, grad_out, logsumexp, doc_ids, inputs, outputs)
    )
    visiting = shifted(keys_values, "context", 1)
    dv_own, turned, q_near, kv_near, lse_near, do_near, docs_near = call(
        functools.partial(own_values, heads, cycle_size, x_size, z_size),
        [
            shape((tok_rows, HD), F32), shape((features, tok_rows), BF16),
            shape(queries.shape, BF16), shape(keys_values.shape, BF16),
            shape(logsumexp.shape, F32), shape(grad_out.shape, BF16),
            shape((2, 1, tok_rows), jnp.int32),
        ],
        [hbm] * 6, 400_000_000, 6_000_000, "own_values",
        scratch=[pltpu.VMEM(inputs.shape, BF16), pltpu.SemaphoreType.DMA((7,))],
    )(
        queries, pltpu.with_memory_space_constraint(keys_values, pltpu.HBM), logsumexp, grad_out,
        doc_ids, inputs,
    )
    (dv_prev,) = call(
        functools.partial(prev_values, heads), [shape((tok_rows, HD), BF16)],
        [vmem] * 5, 300_000_000, 1_200_000, "prev_values",
    )(q_near, visiting, lse_near, do_near, docs_near)
    dv_back = shifted(dv_prev, "context", -1)
    partial, dv_half = call(
        project, [shape((features, HD), BF16), shape((tok_rows, HD), BF16)],
        [vmem] * 3, 300_000_000, 3_000_000, "project",
        scratch=[pltpu.VMEM((features, HD), BF16), pltpu.SemaphoreType.DMA((8,))], out_places=[hbm, vmem],
    )(turned, dv_own, dv_back)
    proj_grad = scattered(partial, x_size, z_size)
    dq, dk_own, dk_prev = call(
        functools.partial(rest, heads),
        [
            shape(queries.shape, BF16), shape((tok_rows, HD), F32), shape((tok_rows, HD), BF16),
        ],
        [vmem] * 7 + [pl.ANY], 2_000_000_000, 3_000_000, "rest",
        scratch=[pltpu.VMEM((tok_rows, HD), F32)],
    )(q_near, kv_near, visiting, lse_near, do_near, outputs, docs_near, dv_half)
    dk_back = shifted(dk_prev, "context", -1)
    dk_half = (dk_own + dk_back.astype(F32)).astype(BF16)
    grad_kv = jnp.concatenate([dk_half, dv_half], axis=1)
    return dq, grad_kv[None], proj_grad[None]


def solution(mesh):
    in_specs = (
        P("dp", "context", "tensor"),
        P("dp", "context", "tensor"),
        P("dp", "context", "tensor"),
        P("dp", "context", "tensor"),
        P("dp", "tensor", "context"),
        P("dp", None),
        P("dp", "context", None),
    )
    out_specs = (
        P("dp", "context", "tensor"),
        P("dp", "context", "tensor"),
        P("tensor", ("context", "dp"), None),
    )
    return jax.shard_map(
        per_device, mesh=mesh, in_specs=in_specs, out_specs=out_specs, check_vma=False
    )
```

```python
import functools
import math

import jax
import jax.numpy as jnp
from jax import lax
from jax.experimental import pallas as pl
from jax.experimental.pallas import tpu as pltpu
from jax.sharding import PartitionSpec as P

HD = 128
HALF = 128
F32 = jnp.float32
BF16 = jnp.bfloat16
LOG2E = 1.0 / math.log(2.0)
SCALING = HD ** -0.5
NT = (((1,), (1,)), ((), ()))
NN = (((1,), (0,)), ((), ()))
TN = (((0,), (0,)), ((), ()))


def dot(a, b, dims):
    return lax.dot_general(a, b, dims, preferred_element_type=F32)


def shifted(block, axis, distance):
    devices = range(lax.axis_size(axis))
    route = [((i - distance) % len(devices), i) for i in devices]
    return lax.ppermute(block, axis, route)


def down(row):
    return jnp.transpose(jnp.broadcast_to(row, (HALF, HALF)))


def halves(docs_ref, stretch):
    row = docs_ref[stretch].astype(F32)
    return row[:, :HALF], row[:, HALF:]


def own_masks(docs_ref):
    early, late = halves(docs_ref, 0)
    early_down, late_down = down(early), down(late)
    causal = lax.broadcasted_iota(jnp.int32, (HALF, HALF), 0) <= lax.broadcasted_iota(
        jnp.int32, (HALF, HALF), 1
    )
    return causal & (early_down == early), early_down == late, causal & (late_down == late)


def prev_masks(docs_ref, is_first):
    early, late = halves(docs_ref, 0)
    key_early, key_late = halves(docs_ref, 1)
    key_other = jnp.where(is_first, key_late, key_early)
    return down(key_early) == late, down(key_other) == jnp.where(is_first, late, early)


def other_offset():
    return pl.multiple_of(jnp.where(lax.axis_index("context") == 0, HALF, 0), HALF)


def prob_of(scores, lse_row, visible):
    return jnp.where(
        visible, jnp.exp2(scores * (SCALING * LOG2E) - lse_row * LOG2E), jnp.float32(0.0)
    )


def swap_order(x_size, z_size):
    odd = lax.rem(lax.axis_index("tensor"), 2)
    return lambda x, z: jnp.where(odd == 0, x * z_size + z, z * x_size + x)


def own_values(
    heads, cycle_size, x_size, z_size, q_hbm, kv_hbm, lse_hbm, do_hbm, docs_hbm, x_hbm,
    dv_ref, xt_ref, q_ref, kv_ref, lse_ref, do_ref, docs_ref, x_ref, sems,
):
    me = lax.axis_index("context")
    prev = lax.rem(me + cycle_size - 1, cycle_size)
    rows = 2 * HALF

    def docs_of(stretch):
        return docs_hbm.at[:, pl.ds(pl.multiple_of(stretch * rows, rows), rows)]

    pairs = [
        (q_hbm, q_ref), (kv_hbm, kv_ref), (lse_hbm, lse_ref), (do_hbm, do_ref),
        (docs_of(me), docs_ref.at[0]), (docs_of(prev), docs_ref.at[1]), (x_hbm, x_ref),
    ]
    copies = [
        pltpu.make_async_copy(source, target, sems.at[i])
        for i, (source, target) in enumerate(pairs)
    ]
    for copy in copies:
        copy.start()
    for copy in copies[:-1]:
        copy.wait()
    see_ee, see_el, see_ll = own_masks(docs_ref)
    key_early, key_late = kv_ref[0, :HALF, :HD], kv_ref[0, HALF:, :HD]
    early = jnp.zeros((HALF, HD), F32)
    late = jnp.zeros((HALF, HD), F32)
    for h in range(heads):
        cols = slice(h * HD, (h + 1) * HD)
        scores_early = dot(key_early, q_ref[0, :, cols], NT)
        scores_late = dot(key_late, q_ref[0, HALF:, cols], NT)
        lse_e, lse_l = lse_ref[0, h : h + 1, :HALF], lse_ref[0, h : h + 1, HALF:]
        prob_early = jnp.concatenate(
            [
                prob_of(scores_early[:, :HALF], lse_e, see_ee).astype(BF16),
                prob_of(scores_early[:, HALF:], lse_l, see_el).astype(BF16),
            ],
            axis=1,
        )
        prob_late = prob_of(scores_late, lse_l, see_ll).astype(BF16)
        early = early + dot(prob_early, do_ref[0, :, cols], NN)
        late = late + dot(prob_late, do_ref[0, HALF:, cols], NN)
    dv_ref[:HALF] = early
    dv_ref[HALF:] = late
    copies[-1].wait()
    place = swap_order(x_size, z_size)
    chunk = x_ref.shape[2] // (x_size * z_size)
    for x in range(x_size):
        wide = chunk * z_size
        turned = jnp.transpose(x_ref[0, :, x * wide : (x + 1) * wide])
        for z in range(z_size):
            start = pl.multiple_of(place(x, z) * chunk, chunk)
            xt_ref[pl.ds(start, chunk)] = turned[z * chunk : (z + 1) * chunk]


def prev_values(heads, q_ref, kv_ref, lse_ref, do_ref, docs_ref, dv_ref):
    is_first = lax.axis_index("context") == 0
    query_row = docs_ref[0].astype(F32)
    key_early, key_late = halves(docs_ref, 1)
    early_down = down(key_early)

    @pl.when(jnp.logical_not(is_first))
    def _():
        visible = jnp.concatenate([early_down, early_down], axis=1) == query_row
        total = jnp.zeros((HALF, HD), F32)
        for h in range(heads):
            cols = slice(h * HD, (h + 1) * HD)
            scores = dot(kv_ref[0, :HALF, :HD], q_ref[0, :, cols], NT)
            prob = prob_of(scores, lse_ref[0, h : h + 1, :], visible).astype(BF16)
            total = total + dot(prob, do_ref[0, :, cols], NN)
        dv_ref[:HALF] = total.astype(BF16)
        dv_ref[HALF:] = jnp.zeros((HALF, HD), BF16)

    @pl.when(is_first)
    def _():
        visible = jnp.concatenate([early_down, down(key_late)], axis=0) == query_row[:, HALF:]
        total = jnp.zeros((2 * HALF, HD), F32)
        for h in range(heads):
            cols = slice(h * HD, (h + 1) * HD)
            scores = dot(kv_ref[0, :, :HD], q_ref[0, HALF:, cols], NT)
            prob = prob_of(scores, lse_ref[0, h : h + 1, HALF:], visible).astype(BF16)
            total = total + dot(prob, do_ref[0, HALF:, cols], NN)
        dv_ref[...] = total.astype(BF16)


def project(xt_ref, own_ref, back_ref, part_hbm, dv_ref, part_ref, sems):
    value_half = (own_ref[...] + back_ref[...].astype(F32)).astype(BF16)
    dv_ref[...] = value_half
    pieces = sems.shape[0]
    rows = part_ref.shape[0] // pieces
    copies = []
    for i in range(pieces):
        piece = slice(i * rows, (i + 1) * rows)
        part_ref[piece] = dot(xt_ref[piece], value_half, NN).astype(BF16)
        copies.append(
            pltpu.make_async_copy(part_ref.at[piece], part_hbm.at[piece], sems.at[i])
        )
        copies[-1].start()
    for copy in copies:
        copy.wait()


def add_up(shares_ref, sum_ref):
    total = shares_ref[0].astype(F32)
    for i in range(1, shares_ref.shape[0]):
        total = total + shares_ref[i].astype(F32)
    sum_ref[...] = total.astype(BF16)


def rest(
    heads, q_ref, kv_ref, prev_ref, lse_ref, do_ref, out_ref, docs_ref, after_ref,
    dq_ref, dk_ref, dk_prev_ref, acc_ref,
):
    offset = other_offset()
    see_ee, see_el, see_ll = own_masks(docs_ref)
    see_pl, see_other = prev_masks(docs_ref, offset > 0)
    key_e, key_l = kv_ref[0, :HALF, :HD], kv_ref[0, HALF:, :HD]
    val_e, val_l = kv_ref[0, :HALF, HD:], kv_ref[0, HALF:, HD:]
    key_p, val_p = prev_ref[0, :HALF, :HD], prev_ref[0, :HALF, HD:]
    key_o, val_o = prev_ref[0, pl.ds(offset, HALF), :HD], prev_ref[0, pl.ds(offset, HALF), HD:]
    lane = lax.broadcasted_iota(jnp.int32, (2 * HALF, HD), 1)
    deltas = jnp.zeros((2 * HALF, HD), F32)
    for h in range(heads):
        cols = slice(h * HD, (h + 1) * HD)
        row_sum = jnp.sum(
            do_ref[0, :, cols].astype(F32) * out_ref[0, :, cols].astype(F32), axis=1, keepdims=True
        )
        deltas = jnp.where(lane == h, row_sum, deltas)
    deltas = jnp.transpose(deltas)
    other_deltas = jnp.where(offset > 0, deltas[:, HALF:], deltas[:, :HALF])
    zero = jnp.zeros((HALF, HD), F32)
    dk_e, dk_l, dk_p, dk_o = zero, zero, zero, zero
    keys_late = jnp.concatenate([key_e, key_l, key_p], axis=0)
    for h in range(heads):
        cols = slice(h * HD, (h + 1) * HD)
        q_h, do_h = q_ref[0, :, cols], do_ref[0, :, cols]
        q_l, do_l = q_ref[0, HALF:, cols], do_ref[0, HALF:, cols]
        q_o, do_o = q_ref[0, pl.ds(offset, HALF), cols], do_ref[0, pl.ds(offset, HALF), cols]
        lse_e, lse_l = lse_ref[0, h : h + 1, :HALF], lse_ref[0, h : h + 1, HALF:]
        lse_o = lse_ref[0, h : h + 1, pl.ds(offset, HALF)]
        delta_e, delta_l = deltas[h : h + 1, :HALF], deltas[h : h + 1, HALF:]
        delta_o = other_deltas[h : h + 1]

        s_e, g_e = dot(key_e, q_h, NT), dot(val_e, do_h, NT)
        ds_ee = (prob_of(s_e[:, :HALF], lse_e, see_ee) * (g_e[:, :HALF] - delta_e)).astype(BF16)
        ds_el = (prob_of(s_e[:, HALF:], lse_l, see_el) * (g_e[:, HALF:] - delta_l)).astype(BF16)
        ds_ll = (
            prob_of(dot(key_l, q_l, NT), lse_l, see_ll) * (dot(val_l, do_l, NT) - delta_l)
        ).astype(BF16)
        ds_pl = (
            prob_of(dot(key_p, q_l, NT), lse_l, see_pl) * (dot(val_p, do_l, NT) - delta_l)
        ).astype(BF16)
        ds_o = (
            prob_of(dot(key_o, q_o, NT), lse_o, see_other) * (dot(val_o, do_o, NT) - delta_o)
        ).astype(BF16)
        dk_e = dk_e + dot(jnp.concatenate([ds_ee, ds_el], axis=1), q_h, NN)
        dk_l = dk_l + dot(ds_ll, q_l, NN)
        dk_p = dk_p + dot(ds_pl, q_l, NN)
        dk_o = dk_o + dot(ds_o, q_o, NN)
        acc_ref[:HALF] = dot(ds_ee, key_e, TN)
        acc_ref[HALF:] = dot(jnp.concatenate([ds_el, ds_ll, ds_pl], axis=0), keys_late, TN)
        acc_ref[pl.ds(offset, HALF)] += dot(ds_o, key_o, TN)
        dq_ref[0, :, cols] = (SCALING * acc_ref[...]).astype(BF16)
    is_first = offset > 0
    dk_ref[:HALF] = SCALING * dk_e
    dk_ref[HALF:] = SCALING * dk_l
    dk_prev_ref[:HALF] = (SCALING * jnp.where(is_first, dk_p, dk_p + dk_o)).astype(BF16)
    dk_prev_ref[HALF:] = (SCALING * jnp.where(is_first, dk_o, zero)).astype(BF16)


def call(body, outs, places, flops, moved, name, scratch=(), out_places=None):
    return pl.pallas_call(
        body,
        out_shape=outs,
        in_specs=[pl.BlockSpec(memory_space=place) for place in places],
        out_specs=[
            pl.BlockSpec(memory_space=place) for place in out_places or [pltpu.VMEM] * len(outs)
        ],
        scratch_shapes=list(scratch),
        compiler_params=pltpu.CompilerParams(vmem_limit_bytes=24 * 1024 * 1024),
        cost_estimate=pl.CostEstimate(flops=flops, bytes_accessed=moved, transcendentals=0),
        name=name,
    )


def sum_over(shares, rows):
    return jnp.sum(shares.reshape(-1, rows, HD).astype(F32), axis=0)


def scattered(partial, x_size, z_size):
    axes = ("context", "dp", "tensor")
    n_dp, n_tensor = lax.axis_size("dp"), lax.axis_size("tensor")

    def index(x, z, d, t):
        return ((x * z_size + z) * n_dp + d) * n_tensor + t

    first, second = [], []
    for t in range(n_tensor):
        x_first = t % 2 == 0
        for fixed in range(x_size if not x_first else z_size):
            for d in range(n_dp):
                first.append(
                    [index(j, fixed, d, t) for j in range(x_size)] if x_first
                    else [index(fixed, j, d, t) for j in range(z_size)]
                )
        for fixed in range(z_size if not x_first else x_size):
            second.append(
                [index(fixed, j, d, t) for j in range(z_size) for d in range(n_dp)] if x_first
                else [index(j, fixed, d, t) for j in range(x_size) for d in range(n_dp)]
            )
    shares = lax.all_to_all(partial, axes, 0, 0, axis_index_groups=first, tiled=True)
    rows = partial.shape[0] // z_size
    (sums,) = call(
        add_up, [jax.ShapeDtypeStruct((rows, HD), BF16)], [pltpu.VMEM], 2_000_000, 1_200_000,
        "add_up",
    )(shares.reshape(z_size, rows, HD))
    shares = lax.all_to_all(sums, axes, 0, 0, axis_index_groups=second, tiled=True)
    return sum_over(shares, sums.shape[0] // (x_size * n_dp))


def per_device(queries, keys_values, outputs, grad_out, logsumexp, doc_ids, inputs):
    tok_rows = queries.shape[1]
    heads = queries.shape[2] // HD
    features = inputs.shape[2]
    cycle_size = lax.axis_size("context")
    x_size = z_size = math.isqrt(cycle_size)
    shape = jax.ShapeDtypeStruct
    hbm, vmem = pltpu.HBM, pltpu.VMEM

    queries, grad_out, logsumexp, doc_ids, inputs, outputs = (
        pltpu.with_memory_space_constraint(a, pltpu.HBM)
        for a in (queries, grad_out, logsumexp, doc_ids, inputs, outputs)
    )
    visiting = shifted(keys_values, "context", 1)
    dv_own, turned, q_near, kv_near, lse_near, do_near, docs_near = call(
        functools.partial(own_values, heads, cycle_size, x_size, z_size),
        [
            shape((tok_rows, HD), F32), shape((features, tok_rows), BF16),
            shape(queries.shape, BF16), shape(keys_values.shape, BF16),
            shape(logsumexp.shape, F32), shape(grad_out.shape, BF16),
            shape((2, 1, tok_rows), jnp.int32),
        ],
        [hbm] * 6, 400_000_000, 6_000_000, "own_values",
        scratch=[pltpu.VMEM(inputs.shape, BF16), pltpu.SemaphoreType.DMA((7,))],
    )(
        queries, pltpu.with_memory_space_constraint(keys_values, pltpu.HBM), logsumexp, grad_out,
        doc_ids, inputs,
    )
    (dv_prev,) = call(
        functools.partial(prev_values, heads), [shape((tok_rows, HD), BF16)],
        [vmem] * 5, 300_000_000, 1_200_000, "prev_values",
    )(q_near, visiting, lse_near, do_near, docs_near)
    dv_back = shifted(dv_prev, "context", -1)
    partial, dv_half = call(
        project, [shape((features, HD), BF16), shape((tok_rows, HD), BF16)],
        [vmem] * 3, 300_000_000, 3_000_000, "project",
        scratch=[pltpu.VMEM((features, HD), BF16), pltpu.SemaphoreType.DMA((16,))], out_places=[hbm, vmem],
    )(turned, dv_own, dv_back)
    proj_grad = scattered(partial, x_size, z_size)
    dq, dk_own, dk_prev = call(
        functools.partial(rest, heads),
        [
            shape(queries.shape, BF16), shape((tok_rows, HD), F32), shape((tok_rows, HD), BF16),
        ],
        [vmem] * 7 + [pl.ANY], 2_000_000_000, 3_000_000, "rest",
        scratch=[pltpu.VMEM((tok_rows, HD), F32)],
    )(q_near, kv_near, visiting, lse_near, do_near, outputs, docs_near, dv_half)
    dk_back = shifted(dk_prev, "context", -1)
    dk_half = (dk_own + dk_back.astype(F32)).astype(BF16)
    grad_kv = jnp.concatenate([dk_half, dv_half], axis=1)
    return dq, grad_kv[None], proj_grad[None]


def solution(mesh):
    in_specs = (
        P("dp", "context", "tensor"),
        P("dp", "context", "tensor"),
        P("dp", "context", "tensor"),
        P("dp", "context", "tensor"),
        P("dp", "tensor", "context"),
        P("dp", None),
        P("dp", "context", None),
    )
    out_specs = (
        P("dp", "context", "tensor"),
        P("dp", "context", "tensor"),
        P("tensor", ("context", "dp"), None),
    )
    return jax.shard_map(
        per_device, mesh=mesh, in_specs=in_specs, out_specs=out_specs, check_vma=False
    )
```
